32 devices in a mesh: seq: 8 (over y, x, core), tp: 4 (over z).
Axes of the slice: x: 2, y: 2, z: 4, core: 2. Of those that a mesh axis runs over, the one named last changes fastest.
Arguments:
- x_codes: int32 [1024, 8192], P('seq', 'tp'), may hold values from -127 to 127
- w_codes: int32 [3, 8192, 8192], P(None, 'tp', 'seq'), may hold values from -127 to 127
- req_mult: int32 [3, 8192], P(None, 'seq'), may hold values from 64 to 255
- req_shift: int32 [3, 8192], P(None, 'seq'), may hold values from 20 to 21
- short_codes: int32 [3, 3, 8192], P(None, None, 'seq'), may hold values from -127 to 127
- residue_codes: int32 [16, 8192], P(None, 'seq'), may hold values from -127 to 127
- rates: float32 [16, 8192], P(None, 'seq'), may hold values from 0.0009765625 to 0.0625
- skip_gain: float32 [8192], P('seq'), may hold values from -4 to 4
Outputs:
- gated: bfloat16 [1024, 8192], P(('seq', 'tp'))
The draws below stay inside these ranges and needn't reach their ends.
All inputs are finite; a program needn't handle non-finite values.
Results may differ from the reference program's by a relative error of at most 0.0057.
Values may be sent and summed in bfloat16 or wider, within the bound.
No kernel may reach another device: no remote copies, remote signals or barrier semaphores. Data moves between devices by JAX's collectives and lax.ppermute only.
A program may use at most 384 MiB of HBM per device.

```python
import math
import jax
import jax.numpy as jnp
from jax import lax

D = 8192
STATES = 16
SHORT = 3
SEQLEN = 1024


def plant(values, key, smallest, top_value):
    place = [jax.random.randint(jax.random.fold_in(key, axis), (), 0, length) for axis, length in enumerate(values.shape)]
    widest = values.shape.index(max(values.shape))
    next_to = place[:widest] + [(place[widest] + 1) % values.shape[widest]] + place[widest + 1:]
    return values.at[tuple(place)].set(smallest).at[tuple(next_to)].set(top_value)


def block_scale(own_key, shape, split, low, top_value):
    def one(position, blocks):
        heights = jax.random.uniform(jax.random.fold_in(jax.random.fold_in(own_key, 6), position), (blocks,), jnp.float32, low / len(split), top_value / len(split))
        return jnp.repeat(jnp.exp(heights), shape[position] // blocks).reshape((-1,) + (1,) * (len(shape) - position - 1))

    gain = one(*split[0])
    for cut in split[1:]:
        gain = gain * one(*cut)
    return gain


def scatter_about(rng, shape, scale, most, pieces=(), kind=jnp.bfloat16):
    values = scale * jax.random.normal(rng, shape, jnp.float32)
    if pieces:
        values = values * block_scale(rng, shape, pieces, -0.22, 0.18)
    return jnp.clip(values, -most, most).astype(kind)


def setup_inputs(seed: int = 0) -> dict:
    streams_of = jax.random.split(jax.random.key(seed), 9)
    x_codes = plant(jax.random.randint(streams_of[0], (SEQLEN, D), -127, 128), jax.random.fold_in(streams_of[0], 1), -127, 127).astype(jnp.int32)
    w_codes = plant(jax.random.randint(streams_of[1], (3, D, D), -127, 128), jax.random.fold_in(streams_of[1], 1), -127, 127).astype(jnp.int32)
    req_mult = plant(jax.random.randint(streams_of[2], (3, D), 64, 256), jax.random.fold_in(streams_of[2], 1), 64, 255).astype(jnp.int32)
    req_shift = plant(jax.random.randint(streams_of[3], (3, D), 20, 22), jax.random.fold_in(streams_of[3], 1), 20, 21).astype(jnp.int32)
    short_codes = plant(jax.random.randint(streams_of[4], (SHORT, 3, D), -127, 128), jax.random.fold_in(streams_of[4], 1), -127, 127).astype(jnp.int32)
    residue_codes = plant(jax.random.randint(streams_of[5], (STATES, D), -127, 128), jax.random.fold_in(streams_of[5], 1), -127, 127).astype(jnp.int32)
    rates = jnp.clip(jnp.exp(math.log(0.0625) - 4.158883 * jax.random.uniform(streams_of[6], (STATES, D), jnp.float32) ** block_scale(streams_of[6], (STATES, D), ((1, 8),), -0.2, 0.2)), 0.0009765625, 0.0625)
    skip_gain = scatter_about(streams_of[7], (D,), 1.0, 4.0, ((0, 8),), jnp.float32)
    return dict(x_codes=x_codes, w_codes=w_codes, req_mult=req_mult, req_shift=req_shift, short_codes=short_codes, residue_codes=residue_codes, rates=rates, skip_gain=skip_gain)


def shifted_lag(values, lag):
    if lag == 0:
        return values
    padded = jnp.pad(values, ((0, 0), (0, 0), (lag, 0)))
    return padded[:, :, :values.shape[2]]

def reference(x_codes, w_codes, req_mult, req_shift, short_codes, residue_codes, rates, skip_gain):
    seqlen = x_codes.shape[0]
    x_float = x_codes.astype(jnp.float32)
    requant = req_mult.astype(jnp.float32) * jnp.exp2(-req_shift.astype(jnp.float32))
    coded_list = []
    for which in range(3):
        summed = jnp.dot(x_float, w_codes[which].astype(jnp.float32), precision=lax.Precision.HIGHEST)
        coded_list.append(jnp.clip(summed * requant[which][None, :], -127.0, 127.0).astype(jnp.bfloat16))
    coded = jnp.stack(coded_list)
    values = jnp.transpose(coded.astype(jnp.float32), (0, 2, 1)) * (1.0 / 64.0)
    short_taps = short_codes.astype(jnp.float32) * (1.0 / 128.0)
    featured = short_taps[0][:, :, None] * shifted_lag(values, 0)
    for lag in range(1, SHORT):
        featured = featured + short_taps[lag][:, :, None] * shifted_lag(values, lag)
    queries = featured[0]
    drive = featured[1] * featured[2]
    coeffs = residue_codes.astype(jnp.float32) * (1.0 / (127.0 * math.sqrt(STATES))) * jnp.sqrt(-jnp.expm1(-2.0 * rates))
    positions = jnp.arange(seqlen).astype(jnp.float32)
    kernel = jnp.zeros(drive.shape, jnp.float32)
    for mode in range(STATES):
        kernel = kernel + coeffs[mode][:, None] * jnp.exp(-rates[mode][:, None] * positions[None, :])
    length_fft = 2 * seqlen
    spectrum = jnp.fft.rfft(drive, length_fft, axis=1) * jnp.fft.rfft(kernel, length_fft, axis=1)
    convolved = jnp.fft.irfft(spectrum, length_fft, axis=1)[:, :seqlen]
    mixed = convolved + skip_gain[:, None] * drive
    gated = (queries * mixed).astype(jnp.bfloat16)
    return jnp.transpose(gated)
```

```python
import functools
import math

import jax
import jax.numpy as jnp
from jax import lax
from jax.experimental import pallas as pl
from jax.experimental.pallas import tpu as pltpu
from jax.sharding import PartitionSpec as P

LANES = 128
WIRE = jnp.float16
WIRE_SCALE = 2.0
OUTER_PAIRS = [(0, 1), (1, 0), (2, 3), (3, 2)]
INNER_PAIRS = [(1, 2), (2, 1)]


def project_kernel(where_ref, x_ref, w_ref, scale_ref, out_ref):
    weights = w_ref[0].astype(jnp.float32).astype(jnp.bfloat16)
    out_ref[...] = (
        jnp.dot(x_ref[...], weights, preferred_element_type=jnp.float32) * scale_ref[0]
    )


def project(rows, w_codes, scale, column_block, width):
    count, features = rows.shape
    kinds = w_codes.shape[0]
    return pl.pallas_call(
        project_kernel,
        grid_spec=pltpu.PrefetchScalarGridSpec(
            num_scalar_prefetch=1,
            grid=(kinds,),
            in_specs=[
                pl.BlockSpec((count, features), lambda k, where: (0, 0)),
                pl.BlockSpec((1, features, width), lambda k, where: (k, 0, where[0])),
                pl.BlockSpec((1, 1, width), lambda k, where: (k, 0, where[0])),
            ],
            out_specs=pl.BlockSpec((count, width), lambda k, where: (0, k)),
        ),
        out_shape=jax.ShapeDtypeStruct((count, kinds * width), jnp.float32),
        compiler_params=pltpu.CompilerParams(vmem_limit_bytes=24 * 2**20),
        cost_estimate=pl.CostEstimate(
            flops=2 * count * features * kinds * width,
            bytes_accessed=4 * features * kinds * width + 4 * count * kinds * width + 2 * count * features,
            transcendentals=0,
        ),
    )(column_block, rows, w_codes, scale)


def conv_kernel(blocks, block_rows, shorts, states, place_ref, query_code_ref, key_code_ref, value_code_ref, taps_ref,
                decay_ref, decay_block_ref, coeff_ref, skip_ref, out_ref, pad_ref, query_ref, drive_ref, mixed_ref,
                sums_ref):
    sublanes = 8
    folds = blocks // sublanes
    place = place_ref[0]
    halo = 8
    for r in range(blocks):
        absolute = lax.bitwise_xor(jnp.int32(r), place)
        before = lax.bitwise_xor(jnp.maximum(absolute - 1, 0), place)
        has_before = jnp.where(absolute > 0, 1.0 / 64.0, 0.0)
        featured = []
        for k, coded_ref in enumerate((query_code_ref, key_code_ref, value_code_ref)):
            tail_start = pl.multiple_of(before * block_rows + block_rows - 16, 16)
            tail = coded_ref[pl.ds(tail_start, 16), :].astype(jnp.float32) * has_before
            pad_ref[k, pl.ds(0, halo), :] = tail[16 - halo:, :]
            now = coded_ref[pl.ds(r * block_rows, block_rows), :].astype(jnp.float32) * (1.0 / 64.0)
            pad_ref[k, pl.ds(halo, block_rows), :] = now
            total = taps_ref[0, pl.ds(k, 1), :] * now
            for lag in range(1, shorts):
                total = total + taps_ref[lag, pl.ds(k, 1), :] * pad_ref[k, pl.ds(halo - lag, block_rows), :]
            featured.append(total)
        query_ref[pl.ds(r * block_rows, block_rows), :] = featured[0]
        drive_ref[pl.ds(r * block_rows, block_rows), :] = featured[1] * featured[2]
    decays = [jnp.broadcast_to(decay_ref[pl.ds(n, 1), :], (sublanes, LANES)) for n in range(states)]
    for fold in range(folds):
        base = fold * sublanes * block_rows

        def local(i, held):
            now = drive_ref[pl.ds(base + i, sublanes, stride=block_rows), :]
            return tuple(held[n] * decays[n] + now for n in range(states))

        zero = jnp.zeros((sublanes, LANES), jnp.float32)
        held = lax.fori_loop(0, block_rows, local, (zero,) * states, unroll=4)
        for n in range(states):
            sums_ref[n, pl.ds(fold * sublanes, sublanes), :] = held[n]
    carry = jnp.zeros((states, LANES), jnp.float32)
    for a in range(blocks):
        r = lax.bitwise_xor(jnp.int32(a), place)
        own = sums_ref[:, pl.ds(r, 1), :].reshape(states, LANES)
        sums_ref[:, pl.ds(r, 1), :] = carry.reshape(states, 1, LANES)
        carry = carry * decay_block_ref[...] + own
    coeffs = [jnp.broadcast_to(coeff_ref[pl.ds(n, 1), :], (sublanes, LANES)) for n in range(states)]
    for fold in range(folds):
        base = fold * sublanes * block_rows

        def whole(i, held):
            now = drive_ref[pl.ds(base + i, sublanes, stride=block_rows), :]
            held = tuple(held[n] * decays[n] + now for n in range(states))
            parts = [held[n] * coeffs[n] for n in range(states)]
            while len(parts) > 1:
                parts = [parts[j] + parts[j + 1] for j in range(0, len(parts), 2)]
            mixed_ref[pl.ds(base + i, sublanes, stride=block_rows), :] = parts[0]
            return held

        start = tuple(sums_ref[n, pl.ds(fold * sublanes, sublanes), :] for n in range(states))
        lax.fori_loop(0, block_rows, whole, start, unroll=4)
    for r in range(blocks):
        rows = pl.ds(r * block_rows, block_rows)
        gated = query_ref[rows, :] * (mixed_ref[rows, :] + skip_ref[...] * drive_ref[rows, :])
        out_ref[lax.bitwise_xor(jnp.int32(r), place)] = gated.astype(jnp.bfloat16)


def hyena(coded, blocks, taps, decay, decay_block, coeff, skip, place, column_start):
    shorts, kinds, _ = taps.shape
    rows, width = coded.shape[0], coded.shape[1] // kinds
    block_rows, states = rows // blocks, decay.shape[0]
    tiles = width // LANES
    scalars = jnp.stack([place, column_start])
    return pl.pallas_call(
        functools.partial(conv_kernel, blocks, block_rows, shorts, states),
        grid_spec=pltpu.PrefetchScalarGridSpec(
            num_scalar_prefetch=1,
            grid=(width // LANES,),
            in_specs=[
                pl.BlockSpec((rows, LANES), lambda c, s: (0, c)),
                pl.BlockSpec((rows, LANES), lambda c, s: (0, tiles + c)),
                pl.BlockSpec((rows, LANES), lambda c, s: (0, 2 * tiles + c)),
                pl.BlockSpec((shorts, kinds, LANES), lambda c, s: (0, 0, s[1] + c)),
                pl.BlockSpec((states, LANES), lambda c, s: (0, s[1] + c)),
                pl.BlockSpec((states, LANES), lambda c, s: (0, s[1] + c)),
                pl.BlockSpec((states, LANES), lambda c, s: (0, s[1] + c)),
                pl.BlockSpec((1, LANES), lambda c, s: (0, s[1] + c)),
            ],
            out_specs=pl.BlockSpec((blocks, block_rows, LANES), lambda c, s: (0, 0, c)),
            scratch_shapes=[
                pltpu.VMEM((3, 8 + block_rows, LANES), jnp.float32),
                pltpu.VMEM((rows, LANES), jnp.float32),
                pltpu.VMEM((rows, LANES), jnp.float32),
                pltpu.VMEM((rows, LANES), jnp.float32),
                pltpu.VMEM((states, blocks, LANES), jnp.float32),
            ],
        ),
        out_shape=jax.ShapeDtypeStruct((blocks, block_rows, width), jnp.bfloat16),
        compiler_params=pltpu.CompilerParams(vmem_limit_bytes=32 * 2**20),
        cost_estimate=pl.CostEstimate(
            flops=6 * rows * width * states, bytes_accessed=8 * rows * width, transcendentals=0
        ),
    )(scalars, coded, coded, coded, taps, decay, decay_block, coeff, skip)


def on_device(x_codes, w_codes, req_mult, req_shift, short_codes, residue_codes, rates, skip_gain):
    seq_devs = lax.axis_size("seq")
    tp_devs = lax.axis_size("tp")
    assert tp_devs == 4
    place = lax.axis_index("seq")
    layer = lax.axis_index("tp")
    outer = (layer == 0) | (layer == 3)
    rows_dev, features = x_codes.shape
    kinds, _, chan_seq = w_codes.shape
    states = rates.shape[0]
    half = chan_seq // 2
    width = math.gcd(half, 256)
    groups = half // width

    def swap(values, mask):
        return lax.ppermute(values, "seq", [(s, s ^ mask) for s in range(seq_devs)])

    own = x_codes.astype(jnp.bfloat16)
    pairs = [jnp.concatenate([own, swap(own, 1)])]
    for mask in range(2, seq_devs, 2):
        far = swap(own, mask)
        pairs.append(jnp.concatenate([far, swap(far, 1)]))

    requant = req_mult.astype(jnp.float32) * jnp.exp2(-req_shift.astype(jnp.float32))
    scale = (requant * WIRE_SCALE).reshape(kinds, 1, chan_seq)
    taps = short_codes.astype(jnp.float32) * (1.0 / 128.0)
    coeff = (
        residue_codes.astype(jnp.float32)
        * (1.0 / (127.0 * math.sqrt(states)))
        * jnp.sqrt(-jnp.expm1(-2.0 * rates))
    )
    decay = jnp.exp(-rates)
    decay_block = jnp.exp(-rates * rows_dev)
    skip = skip_gain.reshape(1, chan_seq)

    pieces = [(g, 0) for g in range(groups)]
    pieces += [(g, q) for g in range(groups) for q in range(1, seq_devs // 2)]
    count = len(pieces)
    half_first = 1 - layer % 2
    half_second = layer % 2

    def partial(index, which):
        g, q = pieces[index]
        block = (which * groups + g).reshape(1).astype(jnp.int32)
        return project(pairs[q], w_codes, scale, block, width)

    first, second = {}, {}
    got_outer, got_inner = {}, {}
    finals = {}
    first[0] = partial(0, half_first)
    gated = [None] * groups
    for t in range(count + 3):
        send_outer = send_inner = None
        if t < count + 2:
            if t < 2:
                send_outer = first[t]
            else:
                send_outer = first[t - 2] + got_inner[t - 1].astype(jnp.float32)
                if t < count:
                    send_outer = jnp.where(outer, first[t], send_outer)
            send_outer = send_outer.astype(WIRE)
        if t >= 1:
            if t < 3:
                mine = second[t - 1]
            elif t <= count:
                mine = jnp.where(outer, second[t - 3], second[t - 1])
            else:
                mine = second[t - 3]
            total = mine + got_outer[t - 1].astype(jnp.float32)
            if t <= count:
                send_inner = total.astype(WIRE)
            if t >= 3:
                finals[t - 3] = jnp.clip(total * (1.0 / WIRE_SCALE), -127.0, 127.0).astype(jnp.bfloat16)
        if send_inner is not None and send_outer is not None:
            send_outer, send_inner = lax.optimization_barrier((send_outer, send_inner))
        if send_outer is not None:
            got_outer[t] = lax.ppermute(send_outer, "tp", OUTER_PAIRS)
        if send_inner is not None:
            got_inner[t] = lax.ppermute(send_inner, "tp", INNER_PAIRS)
        if t + 1 < count:
            first[t + 1] = partial(t + 1, half_first)
        if t < count:
            second[t] = partial(t, half_second)
        for g in range(groups):
            members = [i for i, piece in enumerate(pieces) if piece[0] == g]
            if t - 3 == members[-1]:
                members = sorted(members, key=lambda i: pieces[i][1])
                coded = jnp.concatenate([finals[i] for i in members])
                column_start = (jnp.where(layer == 0, 0, groups) + g) * (width // LANES)
                gated[g] = hyena(coded, seq_devs, taps, decay, decay_block, coeff, skip, place, column_start)

    rows_out = rows_dev // tp_devs
    mine = jnp.concatenate(gated, axis=2).reshape(seq_devs * tp_devs, rows_out, half)
    spread = lax.all_to_all(mine, ("seq", "tp"), split_axis=0, concat_axis=0, tiled=True)
    spread = spread.reshape(seq_devs, tp_devs, rows_out, half)
    spread = jnp.stack([spread[:, 0], spread[:, 3]], axis=1)
    return jnp.transpose(spread, (2, 0, 1, 3)).reshape(rows_out, seq_devs * chan_seq)


def solution(mesh):
    placed = (
        P("seq", "tp"),
        P(None, "tp", "seq"),
        P(None, "seq"),
        P(None, "seq"),
        P(None, None, "seq"),
        P(None, "seq"),
        P(None, "seq"),
        P("seq"),
    )
    return jax.shard_map(
        on_device, mesh=mesh, in_specs=placed, out_specs=P(("seq", "tp"), None), check_vma=False
    )
```

```python
import functools
import math

import jax
import jax.numpy as jnp
from jax import lax
from jax.experimental import pallas as pl
from jax.experimental.pallas import tpu as pltpu
from jax.sharding import PartitionSpec as P

LANES = 128
WIRE = jnp.float16
WIRE_SCALE = 2.0
OUTER_PAIRS = [(0, 1), (1, 0), (2, 3), (3, 2)]
INNER_PAIRS = [(1, 2), (2, 1)]


ANYWHERE = pl.BlockSpec(memory_space=pl.ANY)


def pass_kernel(value_ref, *refs):
    pass


def after(value, token):
    return pl.pallas_call(
        pass_kernel,
        in_specs=[ANYWHERE, ANYWHERE],
        out_specs=ANYWHERE,
        out_shape=jax.ShapeDtypeStruct(value.shape, value.dtype),
        input_output_aliases={0: 0},
    )(value, token)


def project_kernel(parts, groups, where_ref, *refs):
    row_refs = refs[:parts]
    w_ref, scale_ref, _ = refs[parts : parts + 3]
    *out_refs, rows_ref = refs[parts + 3 :]

    @pl.when(pl.program_id(0) == 0)
    def assemble():
        size = row_refs[0].shape[0]
        for i, row_ref in enumerate(row_refs):
            rows_ref[pl.ds(i * size, size), :] = row_ref[...]

    width = w_ref.shape[2] // groups
    count = out_refs[0].shape[0]
    for g in range(groups):
        columns = slice(g * width, (g + 1) * width)
        weights = w_ref[0, :, columns].astype(jnp.float32).astype(jnp.bfloat16)
        sums = jnp.dot(rows_ref[...], weights, preferred_element_type=jnp.float32) * scale_ref[0, :, columns]
        for i, out_ref in enumerate(out_refs[g::groups]):
            out_ref[...] = sums[i * count : (i + 1) * count]


def project(blocks, w_codes, scale, block, groups, width, token):
    size, features = blocks[0].shape
    count = size * len(blocks)
    outs = groups * len(blocks) // 2
    kinds = w_codes.shape[0]
    columns = groups * width
    return pl.pallas_call(
        functools.partial(project_kernel, len(blocks), groups),
        grid_spec=pltpu.PrefetchScalarGridSpec(
            num_scalar_prefetch=1,
            grid=(kinds,),
            in_specs=[pl.BlockSpec((size, features), lambda k, where: (0, 0))] * len(blocks)
            + [
                pl.BlockSpec((1, features, columns), lambda k, where: (k, 0, where[0])),
                pl.BlockSpec((1, 1, columns), lambda k, where: (k, 0, where[0])),
                ANYWHERE,
            ],
            out_specs=[pl.BlockSpec((2 * size, width), lambda k, where: (0, k))] * outs,
            scratch_shapes=[pltpu.VMEM((count, features), jnp.bfloat16)],
        ),
        out_shape=[jax.ShapeDtypeStruct((2 * size, kinds * width), jnp.float32)] * outs,
        compiler_params=pltpu.CompilerParams(vmem_limit_bytes=48 * 2**20),
        cost_estimate=pl.CostEstimate(flops=1, bytes_accessed=1, transcendentals=0),
    )(
        block.reshape(1).astype(jnp.int32),
        *blocks,
        pltpu.with_memory_space_constraint(w_codes, pltpu.HBM),
        scale,
        token,
    )


def conv_kernel(blocks, block_rows, shorts, states, place_ref, query_code_ref, key_code_ref, value_code_ref, taps_ref,
                decay_ref, decay_block_ref, coeff_ref, skip_ref, out_ref, pad_ref, query_ref, drive_ref, mixed_ref,
                sums_ref):
    sublanes = 8
    folds = blocks // sublanes
    place = place_ref[0]
    halo = 8
    for r in range(blocks):
        absolute = lax.bitwise_xor(jnp.int32(r), place)
        before = lax.bitwise_xor(jnp.maximum(absolute - 1, 0), place)
        has_before = jnp.where(absolute > 0, 1.0 / 64.0, 0.0)
        featured = []
        for k, coded_ref in enumerate((query_code_ref, key_code_ref, value_code_ref)):
            tail_start = pl.multiple_of(before * block_rows + block_rows - 16, 16)
            tail = coded_ref[pl.ds(tail_start, 16), :].astype(jnp.float32) * has_before
            pad_ref[k, pl.ds(0, halo), :] = tail[16 - halo:, :]
            now = coded_ref[pl.ds(r * block_rows, block_rows), :].astype(jnp.float32) * (1.0 / 64.0)
            pad_ref[k, pl.ds(halo, block_rows), :] = now
            total = taps_ref[0, pl.ds(k, 1), :] * now
            for lag in range(1, shorts):
                total = total + taps_ref[lag, pl.ds(k, 1), :] * pad_ref[k, pl.ds(halo - lag, block_rows), :]
            featured.append(total)
        query_ref[pl.ds(r * block_rows, block_rows), :] = featured[0]
        drive_ref[pl.ds(r * block_rows, block_rows), :] = featured[1] * featured[2]
    decays = [jnp.broadcast_to(decay_ref[pl.ds(n, 1), :], (sublanes, LANES)) for n in range(states)]
    for fold in range(folds):
        base = fold * sublanes * block_rows

        def local(i, held):
            now = drive_ref[pl.ds(base + i, sublanes, stride=block_rows), :]
            return tuple(held[n] * decays[n] + now for n in range(states))

        zero = jnp.zeros((sublanes, LANES), jnp.float32)
        held = lax.fori_loop(0, block_rows, local, (zero,) * states, unroll=4)
        for n in range(states):
            sums_ref[n, pl.ds(fold * sublanes, sublanes), :] = held[n]
    carry = jnp.zeros((states, LANES), jnp.float32)
    for a in range(blocks):
        r = lax.bitwise_xor(jnp.int32(a), place)
        own = sums_ref[:, pl.ds(r, 1), :].reshape(states, LANES)
        sums_ref[:, pl.ds(r, 1), :] = carry.reshape(states, 1, LANES)
        carry = carry * decay_block_ref[...] + own
    coeffs = [jnp.broadcast_to(coeff_ref[pl.ds(n, 1), :], (sublanes, LANES)) for n in range(states)]
    for fold in range(folds):
        base = fold * sublanes * block_rows

        def whole(i, held):
            now = drive_ref[pl.ds(base + i, sublanes, stride=block_rows), :]
            held = tuple(held[n] * decays[n] + now for n in range(states))
            parts = [held[n] * coeffs[n] for n in range(states)]
            while len(parts) > 1:
                parts = [parts[j] + parts[j + 1] for j in range(0, len(parts), 2)]
            mixed_ref[pl.ds(base + i, sublanes, stride=block_rows), :] = parts[0]
            return held

        start = tuple(sums_ref[n, pl.ds(fold * sublanes, sublanes), :] for n in range(states))
        lax.fori_loop(0, block_rows, whole, start, unroll=4)
    for r in range(blocks):
        rows = pl.ds(r * block_rows, block_rows)
        gated = query_ref[rows, :] * (mixed_ref[rows, :] + skip_ref[...] * drive_ref[rows, :])
        out_ref[lax.bitwise_xor(jnp.int32(r), place)] = gated.astype(jnp.bfloat16)


def hyena(coded, blocks, taps, decay, decay_block, coeff, skip, place, column_start):
    shorts, kinds, _ = taps.shape
    rows, width = coded.shape[0], coded.shape[1] // kinds
    block_rows, states = rows // blocks, decay.shape[0]
    tiles = width // LANES
    scalars = jnp.stack([place, column_start])
    return pl.pallas_call(
        functools.partial(conv_kernel, blocks, block_rows, shorts, states),
        grid_spec=pltpu.PrefetchScalarGridSpec(
            num_scalar_prefetch=1,
            grid=(width // LANES,),
            in_specs=[
                pl.BlockSpec((rows, LANES), lambda c, s: (0, c)),
                pl.BlockSpec((rows, LANES), lambda c, s: (0, tiles + c)),
                pl.BlockSpec((rows, LANES), lambda c, s: (0, 2 * tiles + c)),
                pl.BlockSpec((shorts, kinds, LANES), lambda c, s: (0, 0, s[1] + c)),
                pl.BlockSpec((states, LANES), lambda c, s: (0, s[1] + c)),
                pl.BlockSpec((states, LANES), lambda c, s: (0, s[1] + c)),
                pl.BlockSpec((states, LANES), lambda c, s: (0, s[1] + c)),
                pl.BlockSpec((1, LANES), lambda c, s: (0, s[1] + c)),
            ],
            out_specs=pl.BlockSpec((blocks, block_rows, LANES), lambda c, s: (0, 0, c)),
            scratch_shapes=[
                pltpu.VMEM((3, 8 + block_rows, LANES), jnp.float32),
                pltpu.VMEM((rows, LANES), jnp.float32),
                pltpu.VMEM((rows, LANES), jnp.float32),
                pltpu.VMEM((rows, LANES), jnp.float32),
                pltpu.VMEM((states, blocks, LANES), jnp.float32),
            ],
        ),
        out_shape=jax.ShapeDtypeStruct((blocks, block_rows, width), jnp.bfloat16),
        compiler_params=pltpu.CompilerParams(vmem_limit_bytes=48 * 2**20),
        cost_estimate=pl.CostEstimate(flops=1, bytes_accessed=1, transcendentals=0),
    )(scalars, coded, coded, coded, taps, decay, decay_block, coeff, skip)


def on_device(x_codes, w_codes, req_mult, req_shift, short_codes, residue_codes, rates, skip_gain):
    seq_devs = lax.axis_size("seq")
    tp_devs = lax.axis_size("tp")
    assert tp_devs == 4
    place = lax.axis_index("seq")
    layer = lax.axis_index("tp")
    outer = (layer == 0) | (layer == 3)
    rows_dev, features = x_codes.shape
    kinds, _, chan_seq = w_codes.shape
    states = rates.shape[0]
    half = chan_seq // 2
    width = math.gcd(half, 256)
    groups = half // width

    def swap(values, mask):
        return lax.ppermute(values, "seq", [(s, s ^ mask) for s in range(seq_devs)])

    own = x_codes.astype(jnp.bfloat16)
    far = {mask: swap(own, mask) for mask in range(2, seq_devs, 2)}
    blocks = {0: own, 1: swap(own, 1)}
    for mask in range(2, seq_devs, 2):
        blocks[mask] = swap(own, mask)
        blocks[mask + 1] = swap(blocks[mask], 1)

    requant = req_mult.astype(jnp.float32) * jnp.exp2(-req_shift.astype(jnp.float32))
    scale = (requant * WIRE_SCALE).reshape(kinds, 1, chan_seq)
    taps = short_codes.astype(jnp.float32) * (1.0 / 128.0)
    coeff = (
        residue_codes.astype(jnp.float32)
        * (1.0 / (127.0 * math.sqrt(states)))
        * jnp.sqrt(-jnp.expm1(-2.0 * rates))
    )
    decay = jnp.exp(-rates)
    decay_block = jnp.exp(-rates * rows_dev)
    skip = skip_gain.reshape(1, chan_seq)

    pairs = list(range(2, seq_devs // 2))
    pieces = [(g, q) for q in (0, 1) for g in range(groups)]
    pieces += [(g, q) for g in range(groups) for q in pairs]
    count = len(pieces)
    half_first = 1 - layer % 2
    half_second = layer % 2

    def partials(store, members, which, token):
        chosen, members = members
        taken = [blocks[2 * q + j] for q in members for j in range(2)]
        block = (which * groups + chosen[0]) // len(chosen)
        results = project(taken, w_codes, scale, block, len(chosen), width, token)
        store.update(zip([pieces.index((g, q)) for q in members for g in chosen], results))

    calls = {pieces.index((0, q)): (list(range(groups)), [q]) for q in (0, 1)}
    for g in range(groups):
        for i in range(0, len(pairs), 2):
            calls[pieces.index((g, pairs[i]))] = [g], pairs[i : i + 2]

    first, second = {}, {}
    got_outer, got_inner = {}, {}
    finals = {}
    token = jnp.zeros((8, LANES), jnp.float32)
    partials(first, calls[0], half_first, token)
    gated = [None] * groups
    ready = [max(i for i, piece in enumerate(pieces) if piece[0] == g) + 3 for g in range(groups)]
    for t in range(count + 3):
        send_outer = send_inner = None
        if t < count + 2:
            if t < 2:
                send_outer = first[t]
            else:
                send_outer = first[t - 2] + got_inner[t - 1].astype(jnp.float32)
                if t < count:
                    send_outer = jnp.where(outer, first[t], send_outer)
            send_outer = send_outer.astype(WIRE)
        if t >= 1:
            if t < 3:
                mine = second[t - 1]
            elif t <= count:
                mine = jnp.where(outer, second[t - 3], second[t - 1])
            else:
                mine = second[t - 3]
            total = mine + got_outer[t - 1].astype(jnp.float32)
            if t <= count:
                send_inner = total.astype(WIRE)
            if t >= 3:
                finals[t - 3] = jnp.clip(total * (1.0 / WIRE_SCALE), -127.0, 127.0).astype(jnp.bfloat16)
        for g in range(groups):
            if t == ready[g] + 1 and send_outer is not None:
                send_outer, gated[g] = lax.optimization_barrier((send_outer, gated[g]))
        if send_inner is not None and send_outer is not None:
            send_outer, send_inner = lax.optimization_barrier((send_outer, send_inner))
        if send_outer is not None:
            got_outer[t] = lax.ppermute(send_outer, "tp", OUTER_PAIRS)
        if send_inner is not None:
            got_inner[t] = lax.ppermute(send_inner, "tp", INNER_PAIRS)
        if t in calls:
            partials(second, calls[t], half_second, blocks.get(6, token) if calls[t][1] == [1] else token)
        if t + 1 in calls:
            partials(first, calls[t + 1], half_first, blocks.get(4, token) if calls[t + 1][1] == [1] else token)
        for g in range(groups):
            members = [i for i, piece in enumerate(pieces) if piece[0] == g]
            if t == ready[g]:
                members = sorted(members, key=lambda i: pieces[i][1])
                coded = jnp.concatenate([finals[i] for i in members])
                column_start = (jnp.where(layer == 0, 0, groups) + g) * (width // LANES)
                gated[g] = hyena(coded, seq_devs, taps, decay, decay_block, coeff, skip, place, column_start)

    rows_out = rows_dev // tp_devs

    def spread(values):
        width = values.shape[2]
        parts = values.reshape(seq_devs, tp_devs, rows_out, width)
        step = jnp.where(layer < 2, 1, -1)

        def slice_for(distance):
            target = jnp.clip(layer + distance * step, 0, tp_devs - 1)
            return lax.dynamic_index_in_dim(parts, target, 1, keepdims=False)

        near = lax.ppermute(slice_for(1), "tp", OUTER_PAIRS)
        middle = lax.ppermute(slice_for(2), "tp", [(0, 2), (2, 0), (1, 3), (3, 1)])
        opposite = lax.ppermute(slice_for(3), "tp", [(0, 3), (3, 0)])
        kept = slice_for(0)
        low = jnp.where(layer == 0, kept, jnp.where(layer == 1, near, jnp.where(layer == 2, middle, opposite)))
        high = jnp.where(layer == 3, kept, jnp.where(layer == 2, near, jnp.where(layer == 1, middle, opposite)))
        return low, high

    halves = [spread(values) for values in gated]
    mine = jnp.concatenate([low for low, _ in halves] + [high for _, high in halves], axis=2)
    landed = lax.all_to_all(mine, "seq", split_axis=0, concat_axis=0, tiled=True)
    return jnp.transpose(landed, (1, 0, 2)).reshape(rows_out, seq_devs * chan_seq)


def solution(mesh):
    placed = (
        P("seq", "tp"),
        P(None, "tp", "seq"),
        P(None, "seq"),
        P(None, "seq"),
        P(None, None, "seq"),
        P(None, "seq"),
        P(None, "seq"),
        P("seq"),
    )
    return jax.shard_map(
        on_device, mesh=mesh, in_specs=placed, out_specs=P(("seq", "tp"), None), check_vma=False
    )
```

```python
import functools
import math

import jax
import jax.numpy as jnp
from jax import lax
from jax.experimental import pallas as pl
from jax.experimental.pallas import tpu as pltpu
from jax.sharding import PartitionSpec as P

LANES = 128
WIRE = jnp.float16
WIRE_SCALE = 2.0
OUTER_PAIRS = [(0, 1), (1, 0), (2, 3), (3, 2)]
INNER_PAIRS = [(1, 2), (2, 1)]


ANYWHERE = pl.BlockSpec(memory_space=pl.ANY)


def pass_kernel(value_ref, *refs):
    pass


def after(value, token):
    return pl.pallas_call(
        pass_kernel,
        in_specs=[ANYWHERE, ANYWHERE],
        out_specs=ANYWHERE,
        out_shape=jax.ShapeDtypeStruct(value.shape, value.dtype),
        input_output_aliases={0: 0},
    )(value, token)


def project_kernel(parts, groups, where_ref, *refs):
    row_refs = refs[:parts]
    w_ref, scale_ref, _ = refs[parts : parts + 3]
    *out_refs, rows_ref = refs[parts + 3 :]

    @pl.when(pl.program_id(0) == 0)
    def assemble():
        size = row_refs[0].shape[0]
        for i, row_ref in enumerate(row_refs):
            rows_ref[pl.ds(i * size, size), :] = row_ref[...]

    width = w_ref.shape[2] // groups
    count = out_refs[0].shape[0]
    for g in range(groups):
        columns = slice(g * width, (g + 1) * width)
        weights = w_ref[0, :, columns].astype(jnp.float32).astype(jnp.bfloat16)
        sums = jnp.dot(rows_ref[...], weights, preferred_element_type=jnp.float32) * scale_ref[0, :, columns]
        start = pl.multiple_of(pl.program_id(0) * width, width)
        for i, out_ref in enumerate(out_refs[g::groups]):
            out_ref[:, pl.ds(start, width)] = sums[i * count : (i + 1) * count]


def project(blocks, w_codes, scale, block, groups, width, token):
    size, features = blocks[0].shape
    count = size * len(blocks)
    outs = groups * len(blocks) // 2
    kinds = w_codes.shape[0]
    columns = groups * width
    return pl.pallas_call(
        functools.partial(project_kernel, len(blocks), groups),
        grid_spec=pltpu.PrefetchScalarGridSpec(
            num_scalar_prefetch=1,
            grid=(kinds,),
            in_specs=[pl.BlockSpec((size, features), lambda k, where: (0, 0))] * len(blocks)
            + [
                pl.BlockSpec((1, features, columns), lambda k, where: (k, 0, where[0])),
                pl.BlockSpec((1, 1, columns), lambda k, where: (k, 0, where[0])),
                ANYWHERE,
            ],
            out_specs=[pl.BlockSpec(memory_space=pltpu.VMEM)] * outs,
            scratch_shapes=[pltpu.VMEM((count, features), jnp.bfloat16)],
        ),
        out_shape=[pltpu.VMEM((2 * size, kinds * width), jnp.float32)] * outs,
        compiler_params=pltpu.CompilerParams(vmem_limit_bytes=24 * 2**20),
        cost_estimate=pl.CostEstimate(flops=1, bytes_accessed=1, transcendentals=0),
    )(
        block.reshape(1).astype(jnp.int32),
        *blocks,
        pltpu.with_memory_space_constraint(w_codes, pltpu.HBM),
        scale,
        token,
    )


def conv_kernel(blocks, block_rows, shorts, states, place_ref, *refs):
    kinds = 3
    code_refs = refs[: kinds * blocks // 2]
    taps_ref, decay_ref, decay_block_ref, coeff_ref, skip_ref, out_ref = refs[len(code_refs) : len(code_refs) + 6]
    pad_ref, query_ref, drive_ref, mixed_ref, sums_ref, tails_ref = refs[len(code_refs) + 6 :]
    sublanes = 8
    folds = blocks // sublanes
    place = place_ref[0]
    halo = 8
    for r in range(blocks):
        for k in range(kinds):
            code_ref = code_refs[r // 2 * kinds + k]
            last = code_ref[pl.ds(r % 2 * block_rows + block_rows - 16, 16), :].astype(jnp.float32)
            tails_ref[r * kinds + k] = last[16 - halo :, :]
    for r in range(blocks):
        absolute = lax.bitwise_xor(jnp.int32(r), place)
        before = lax.bitwise_xor(jnp.maximum(absolute - 1, 0), place)
        has_before = jnp.where(absolute > 0, 1.0 / 64.0, 0.0)
        featured = []
        for k in range(kinds):
            code_ref = code_refs[r // 2 * kinds + k]
            pad_ref[k, pl.ds(0, halo), :] = tails_ref[before * kinds + k] * has_before
            now = code_ref[pl.ds(r % 2 * block_rows, block_rows), :].astype(jnp.float32) * (1.0 / 64.0)
            pad_ref[k, pl.ds(halo, block_rows), :] = now
            total = taps_ref[0, pl.ds(k, 1), :] * now
            for lag in range(1, shorts):
                total = total + taps_ref[lag, pl.ds(k, 1), :] * pad_ref[k, pl.ds(halo - lag, block_rows), :]
            featured.append(total)
        query_ref[pl.ds(r * block_rows, block_rows), :] = featured[0]
        drive_ref[pl.ds(r * block_rows, block_rows), :] = featured[1] * featured[2]
    decays = [jnp.broadcast_to(decay_ref[pl.ds(n, 1), :], (sublanes, LANES)) for n in range(states)]
    for fold in range(folds):
        base = fold * sublanes * block_rows

        def local(i, held):
            now = drive_ref[pl.ds(base + i, sublanes, stride=block_rows), :]
            return tuple(held[n] * decays[n] + now for n in range(states))

        zero = jnp.zeros((sublanes, LANES), jnp.float32)
        held = lax.fori_loop(0, block_rows, local, (zero,) * states, unroll=8)
        for n in range(states):
            sums_ref[n, pl.ds(fold * sublanes, sublanes), :] = held[n]
    carry = jnp.zeros((states, LANES), jnp.float32)
    for a in range(blocks):
        r = lax.bitwise_xor(jnp.int32(a), place)
        own = sums_ref[:, pl.ds(r, 1), :].reshape(states, LANES)
        sums_ref[:, pl.ds(r, 1), :] = carry.reshape(states, 1, LANES)
        carry = carry * decay_block_ref[...] + own
    coeffs = [jnp.broadcast_to(coeff_ref[pl.ds(n, 1), :], (sublanes, LANES)) for n in range(states)]
    for fold in range(folds):
        base = fold * sublanes * block_rows

        def whole(i, held):
            now = drive_ref[pl.ds(base + i, sublanes, stride=block_rows), :]
            held = tuple(held[n] * decays[n] + now for n in range(states))
            parts = [held[n] * coeffs[n] for n in range(states)]
            while len(parts) > 1:
                parts = [parts[j] + parts[j + 1] for j in range(0, len(parts), 2)]
            mixed_ref[pl.ds(base + i, sublanes, stride=block_rows), :] = parts[0]
            return held

        start = tuple(sums_ref[n, pl.ds(fold * sublanes, sublanes), :] for n in range(states))
        lax.fori_loop(0, block_rows, whole, start, unroll=8)
    for r in range(blocks):
        rows = pl.ds(r * block_rows, block_rows)
        gated = query_ref[rows, :] * (mixed_ref[rows, :] + skip_ref[...] * drive_ref[rows, :])
        out_ref[lax.bitwise_xor(jnp.int32(r), place)] = gated.astype(jnp.bfloat16)


def hyena(coded, blocks, taps, decay, decay_block, coeff, skip, place, column_start):
    shorts, kinds, _ = taps.shape
    rows, width = coded[0].shape[0] * len(coded), coded[0].shape[1] // kinds
    block_rows, states = rows // blocks, decay.shape[0]
    tiles = width // LANES
    scalars = jnp.stack([place, column_start])

    def code_spec(k):
        return pl.BlockSpec((2 * block_rows, LANES), lambda c, s: (0, k * tiles + c))

    return pl.pallas_call(
        functools.partial(conv_kernel, blocks, block_rows, shorts, states),
        grid_spec=pltpu.PrefetchScalarGridSpec(
            num_scalar_prefetch=1,
            grid=(width // LANES,),
            in_specs=[
                *[code_spec(k) for _ in coded for k in range(kinds)],
                pl.BlockSpec((shorts, kinds, LANES), lambda c, s: (0, 0, s[1] + c)),
                pl.BlockSpec((states, LANES), lambda c, s: (0, s[1] + c)),
                pl.BlockSpec((states, LANES), lambda c, s: (0, s[1] + c)),
                pl.BlockSpec((states, LANES), lambda c, s: (0, s[1] + c)),
                pl.BlockSpec((1, LANES), lambda c, s: (0, s[1] + c)),
            ],
            out_specs=pl.BlockSpec((blocks, block_rows, LANES), lambda c, s: (0, 0, c)),
            scratch_shapes=[
                pltpu.VMEM((3, 8 + block_rows, LANES), jnp.float32),
                pltpu.VMEM((rows, LANES), jnp.float32),
                pltpu.VMEM((rows, LANES), jnp.float32),
                pltpu.VMEM((rows, LANES), jnp.float32),
                pltpu.VMEM((states, blocks, LANES), jnp.float32),
                pltpu.VMEM((blocks * kinds, 8, LANES), jnp.float32),
            ],
        ),
        out_shape=jax.ShapeDtypeStruct((blocks, block_rows, width), jnp.bfloat16),
        compiler_params=pltpu.CompilerParams(vmem_limit_bytes=24 * 2**20),
        cost_estimate=pl.CostEstimate(flops=1, bytes_accessed=1, transcendentals=0),
    )(scalars, *[piece for piece in coded for _ in range(kinds)], taps, decay, decay_block, coeff, skip)


def on_device(x_codes, w_codes, req_mult, req_shift, short_codes, residue_codes, rates, skip_gain):
    seq_devs = lax.axis_size("seq")
    tp_devs = lax.axis_size("tp")
    assert tp_devs == 4
    place = lax.axis_index("seq")
    layer = lax.axis_index("tp")
    outer = (layer == 0) | (layer == 3)
    rows_dev, features = x_codes.shape
    kinds, _, chan_seq = w_codes.shape
    states = rates.shape[0]
    half = chan_seq // 2
    width = math.gcd(half, 256)
    groups = half // width

    def swap(values, mask):
        return lax.ppermute(values, "seq", [(s, s ^ mask) for s in range(seq_devs)])

    own = x_codes.astype(jnp.bfloat16)
    far = {mask: swap(own, mask) for mask in range(2, seq_devs, 2)}
    blocks = {0: own, 1: swap(own, 1)}
    for mask in range(2, seq_devs, 2):
        blocks[mask] = swap(own, mask)
        blocks[mask + 1] = swap(blocks[mask], 1)

    requant = req_mult.astype(jnp.float32) * jnp.exp2(-req_shift.astype(jnp.float32))
    scale = (requant * WIRE_SCALE).reshape(kinds, 1, chan_seq)
    taps = short_codes.astype(jnp.float32) * (1.0 / 128.0)
    coeff = (
        residue_codes.astype(jnp.float32)
        * (1.0 / (127.0 * math.sqrt(states)))
        * jnp.sqrt(-jnp.expm1(-2.0 * rates))
    )
    decay = jnp.exp(-rates)
    decay_block = jnp.exp(-rates * rows_dev)
    skip = skip_gain.reshape(1, chan_seq)

    pairs = list(range(2, seq_devs // 2))
    pieces = [(g, q) for q in (0, 1) for g in range(groups)]
    pieces += [(g, q) for g in range(groups) for q in pairs]
    count = len(pieces)
    half_first = 1 - layer % 2
    half_second = layer % 2

    def partials(store, members, which, token):
        chosen, members = members
        taken = [blocks[2 * q + j] for q in members for j in range(2)]
        block = (which * groups + chosen[0]) // len(chosen)
        results = project(taken, w_codes, scale, block, len(chosen), width, token)
        store.update(zip([pieces.index((g, q)) for q in members for g in chosen], results))

    calls = {pieces.index((0, q)): (list(range(groups)), [q]) for q in (0, 1)}
    for g in range(groups):
        for i in range(0, len(pairs), 2):
            calls[pieces.index((g, pairs[i]))] = [g], pairs[i : i + 2]

    first, second = {}, {}
    got_outer, got_inner = {}, {}
    finals = {}
    token = jnp.zeros((8, LANES), jnp.float32)
    partials(first, calls[0], half_first, token)
    gated = [None] * groups
    ready = [max(i for i, piece in enumerate(pieces) if piece[0] == g) + 3 for g in range(groups)]
    for t in range(count + 3):
        send_outer = send_inner = None
        if t < count + 2:
            if t < 2:
                send_outer = first[t]
            else:
                send_outer = first[t - 2] + got_inner[t - 1].astype(jnp.float32)
                if t < count:
                    send_outer = jnp.where(outer, first[t], send_outer)
            send_outer = send_outer.astype(WIRE)
        if t >= 1:
            if t < 3:
                mine = second[t - 1]
            elif t <= count:
                mine = jnp.where(outer, second[t - 3], second[t - 1])
            else:
                mine = second[t - 3]
            total = mine + got_outer[t - 1].astype(jnp.float32)
            if t <= count:
                send_inner = total.astype(WIRE)
            if t >= 3:
                finals[t - 3] = jnp.clip(total * (1.0 / WIRE_SCALE), -127.0, 127.0).astype(jnp.bfloat16)
        for g in range(groups):
            if t == ready[g] + 1 and send_outer is not None:
                send_outer, gated[g] = lax.optimization_barrier((send_outer, gated[g]))
        if send_inner is not None and send_outer is not None:
            send_outer, send_inner = lax.optimization_barrier((send_outer, send_inner))
        if send_outer is not None:
            got_outer[t] = lax.ppermute(send_outer, "tp", OUTER_PAIRS)
        if send_inner is not None:
            got_inner[t] = lax.ppermute(send_inner, "tp", INNER_PAIRS)
        if t in calls:
            partials(second, calls[t], half_second, blocks.get(6, token) if calls[t][1] == [1] else token)
        if t + 1 in calls:
            partials(first, calls[t + 1], half_first, blocks.get(4, token) if calls[t + 1][1] == [1] else token)
        for g in range(groups):
            members = [i for i, piece in enumerate(pieces) if piece[0] == g]
            if t == ready[g]:
                members = sorted(members, key=lambda i: pieces[i][1])
                coded = [finals[i] for i in members]
                column_start = (jnp.where(layer == 0, 0, groups) + g) * (width // LANES)
                gated[g] = hyena(coded, seq_devs, taps, decay, decay_block, coeff, skip, place, column_start)

    rows_out = rows_dev // tp_devs

    def spread(values):
        width = values.shape[2]
        parts = values.reshape(seq_devs, tp_devs, rows_out, width)
        step = jnp.where(layer < 2, 1, -1)

        def slice_for(distance):
            target = jnp.clip(layer + distance * step, 0, tp_devs - 1)
            return lax.dynamic_index_in_dim(parts, target, 1, keepdims=False)

        near = lax.ppermute(slice_for(1), "tp", OUTER_PAIRS)
        middle = lax.ppermute(slice_for(2), "tp", [(0, 2), (2, 0), (1, 3), (3, 1)])
        opposite = lax.ppermute(slice_for(3), "tp", [(0, 3), (3, 0)])
        kept = slice_for(0)
        low = jnp.where(layer == 0, kept, jnp.where(layer == 1, near, jnp.where(layer == 2, middle, opposite)))
        high = jnp.where(layer == 3, kept, jnp.where(layer == 2, near, jnp.where(layer == 1, middle, opposite)))
        return low, high

    halves = [spread(values) for values in gated]
    mine = jnp.concatenate([low for low, _ in halves] + [high for _, high in halves], axis=2)
    landed = lax.all_to_all(mine, "seq", split_axis=0, concat_axis=0, tiled=True)
    return jnp.transpose(landed, (1, 0, 2)).reshape(rows_out, seq_devs * chan_seq)


def solution(mesh):
    placed = (
        P("seq", "tp"),
        P(None, "tp", "seq"),
        P(None, "seq"),
        P(None, "seq"),
        P(None, None, "seq"),
        P(None, "seq"),
        P(None, "seq"),
        P("seq"),
    )
    return jax.shard_map(
        on_device, mesh=mesh, in_specs=placed, out_specs=P(("seq", "tp"), None), check_vma=False
    )
```

```python
import functools
import math

import jax
import jax.numpy as jnp
from jax import lax
from jax.experimental import pallas as pl
from jax.experimental.pallas import tpu as pltpu
from jax.sharding import PartitionSpec as P

LANES = 128
WIRE = jnp.float16
WIRE_SCALE = 2.0
OUTER_PAIRS = [(0, 1), (1, 0), (2, 3), (3, 2)]
INNER_PAIRS = [(1, 2), (2, 1)]


ANYWHERE = pl.BlockSpec(memory_space=pl.ANY)


def pass_kernel(value_ref, *refs):
    pass


def after(value, token):
    return pl.pallas_call(
        pass_kernel,
        in_specs=[ANYWHERE, ANYWHERE],
        out_specs=ANYWHERE,
        out_shape=jax.ShapeDtypeStruct(value.shape, value.dtype),
        input_output_aliases={0: 0},
    )(value, token)


def project_kernel(parts, groups, where_ref, *refs):
    row_refs = refs[:parts]
    w_ref, scale_ref, _ = refs[parts : parts + 3]
    *out_refs, rows_ref = refs[parts + 3 :]

    @pl.when(pl.program_id(0) == 0)
    def assemble():
        size = row_refs[0].shape[0]
        for i, row_ref in enumerate(row_refs):
            rows_ref[pl.ds(i * size, size), :] = row_ref[...]

    width = w_ref.shape[2] // groups
    count = out_refs[0].shape[0]
    for g in range(groups):
        columns = slice(g * width, (g + 1) * width)
        weights = w_ref[0, :, columns].astype(jnp.float32).astype(jnp.bfloat16)
        sums = jnp.dot(rows_ref[...], weights, preferred_element_type=jnp.float32) * scale_ref[0, :, columns]
        start = pl.multiple_of(pl.program_id(0) * width, width)
        for i, out_ref in enumerate(out_refs[g::groups]):
            out_ref[:, pl.ds(start, width)] = sums[i * count : (i + 1) * count]


def project(blocks, w_codes, scale, block, groups, width, token):
    size, features = blocks[0].shape
    count = size * len(blocks)
    outs = groups * len(blocks) // 2
    kinds = w_codes.shape[0]
    columns = groups * width
    return pl.pallas_call(
        functools.partial(project_kernel, len(blocks), groups),
        grid_spec=pltpu.PrefetchScalarGridSpec(
            num_scalar_prefetch=1,
            grid=(kinds,),
            in_specs=[pl.BlockSpec((size, features), lambda k, where: (0, 0))] * len(blocks)
            + [
                pl.BlockSpec((1, features, columns), lambda k, where: (k, 0, where[0])),
                pl.BlockSpec((1, 1, columns), lambda k, where: (k, 0, where[0])),
                ANYWHERE,
            ],
            out_specs=[pl.BlockSpec(memory_space=pltpu.VMEM)] * outs,
            scratch_shapes=[pltpu.VMEM((count, features), jnp.bfloat16)],
        ),
        out_shape=[pltpu.VMEM((2 * size, kinds * width), jnp.float32)] * outs,
        compiler_params=pltpu.CompilerParams(vmem_limit_bytes=24 * 2**20),
        cost_estimate=pl.CostEstimate(flops=1, bytes_accessed=1, transcendentals=0),
    )(
        block.reshape(1).astype(jnp.int32),
        *blocks,
        pltpu.with_memory_space_constraint(w_codes, pltpu.HBM),
        scale,
        token,
    )


def conv_kernel(blocks, block_rows, shorts, states, place_ref, *refs):
    kinds = 3
    code_refs = refs[: kinds * blocks // 2]
    taps_ref, decay_ref, decay_block_ref, coeff_ref, skip_ref, out_ref = refs[len(code_refs) : len(code_refs) + 6]
    pad_ref, query_ref, drive_ref, mixed_ref, sums_ref, tails_ref = refs[len(code_refs) + 6 :]
    sublanes = 8
    folds = blocks // sublanes
    place = place_ref[0]
    halo = 8
    for r in range(blocks):
        for k in range(kinds):
            code_ref = code_refs[r // 2 * kinds + k]
            last = code_ref[pl.ds(r % 2 * block_rows + block_rows - 16, 16), :].astype(jnp.float32)
            tails_ref[r * kinds + k] = last[16 - halo :, :]
    for r in range(blocks):
        absolute = lax.bitwise_xor(jnp.int32(r), place)
        before = lax.bitwise_xor(jnp.maximum(absolute - 1, 0), place)
        has_before = jnp.where(absolute > 0, 1.0 / 64.0, 0.0)
        featured = []
        for k in range(kinds):
            code_ref = code_refs[r // 2 * kinds + k]
            pad_ref[k, pl.ds(0, halo), :] = tails_ref[before * kinds + k] * has_before
            now = code_ref[pl.ds(r % 2 * block_rows, block_rows), :].astype(jnp.float32) * (1.0 / 64.0)
            pad_ref[k, pl.ds(halo, block_rows), :] = now
            total = taps_ref[0, pl.ds(k, 1), :] * now
            for lag in range(1, shorts):
                total = total + taps_ref[lag, pl.ds(k, 1), :] * pad_ref[k, pl.ds(halo - lag, block_rows), :]
            featured.append(total)
        query_ref[pl.ds(r * block_rows, block_rows), :] = featured[0]
        drive_ref[pl.ds(r * block_rows, block_rows), :] = featured[1] * featured[2]
    decays = [jnp.broadcast_to(decay_ref[pl.ds(n, 1), :], (sublanes, LANES)) for n in range(states)]
    for fold in range(folds):
        base = fold * sublanes * block_rows

        def local(i, held):
            now = drive_ref[pl.ds(base + i, sublanes, stride=block_rows), :]
            return tuple(held[n] * decays[n] + now for n in range(states))

        zero = jnp.zeros((sublanes, LANES), jnp.float32)
        held = lax.fori_loop(0, block_rows, local, (zero,) * states, unroll=8)
        for n in range(states):
            sums_ref[n, pl.ds(fold * sublanes, sublanes), :] = held[n]
    carry = jnp.zeros((states, LANES), jnp.float32)
    for a in range(blocks):
        r = lax.bitwise_xor(jnp.int32(a), place)
        own = sums_ref[:, pl.ds(r, 1), :].reshape(states, LANES)
        sums_ref[:, pl.ds(r, 1), :] = carry.reshape(states, 1, LANES)
        carry = carry * decay_block_ref[...] + own
    coeffs = [jnp.broadcast_to(coeff_ref[pl.ds(n, 1), :], (sublanes, LANES)) for n in range(states)]
    for fold in range(folds):
        base = fold * sublanes * block_rows

        def whole(i, held):
            now = drive_ref[pl.ds(base + i, sublanes, stride=block_rows), :]
            held = tuple(held[n] * decays[n] + now for n in range(states))
            parts = [held[n] * coeffs[n] for n in range(states)]
            while len(parts) > 1:
                parts = [parts[j] + parts[j + 1] for j in range(0, len(parts), 2)]
            mixed_ref[pl.ds(base + i, sublanes, stride=block_rows), :] = parts[0]
            return held

        start = tuple(sums_ref[n, pl.ds(fold * sublanes, sublanes), :] for n in range(states))
        lax.fori_loop(0, block_rows, whole, start, unroll=8)
    for r in range(blocks):
        rows = pl.ds(r * block_rows, block_rows)
        gated = query_ref[rows, :] * (mixed_ref[rows, :] + skip_ref[...] * drive_ref[rows, :])
        out_ref[lax.bitwise_xor(jnp.int32(r), place)] = gated.astype(jnp.bfloat16)


def hyena(coded, blocks, taps, decay, decay_block, coeff, skip, place, column_start):
    shorts, kinds, _ = taps.shape
    rows, width = coded[0].shape[0] * len(coded), coded[0].shape[1] // kinds
    block_rows, states = rows // blocks, decay.shape[0]
    tiles = width // LANES
    scalars = jnp.stack([place, column_start])

    def code_spec(k):
        return pl.BlockSpec((2 * block_rows, LANES), lambda c, s: (0, k * tiles + c))

    return pl.pallas_call(
        functools.partial(conv_kernel, blocks, block_rows, shorts, states),
        grid_spec=pltpu.PrefetchScalarGridSpec(
            num_scalar_prefetch=1,
            grid=(width // LANES,),
            in_specs=[
                *[code_spec(k) for _ in coded for k in range(kinds)],
                pl.BlockSpec((shorts, kinds, LANES), lambda c, s: (0, 0, s[1] + c)),
                pl.BlockSpec((states, LANES), lambda c, s: (0, s[1] + c)),
                pl.BlockSpec((states, LANES), lambda c, s: (0, s[1] + c)),
                pl.BlockSpec((states, LANES), lambda c, s: (0, s[1] + c)),
                pl.BlockSpec((1, LANES), lambda c, s: (0, s[1] + c)),
            ],
            out_specs=pl.BlockSpec((blocks, block_rows, LANES), lambda c, s: (0, 0, c)),
            scratch_shapes=[
                pltpu.VMEM((3, 8 + block_rows, LANES), jnp.float32),
                pltpu.VMEM((rows, LANES), jnp.float32),
                pltpu.VMEM((rows, LANES), jnp.float32),
                pltpu.VMEM((rows, LANES), jnp.float32),
                pltpu.VMEM((states, blocks, LANES), jnp.float32),
                pltpu.VMEM((blocks * kinds, 8, LANES), jnp.float32),
            ],
        ),
        out_shape=jax.ShapeDtypeStruct((blocks, block_rows, width), jnp.bfloat16),
        compiler_params=pltpu.CompilerParams(vmem_limit_bytes=24 * 2**20),
        cost_estimate=pl.CostEstimate(flops=1, bytes_accessed=1, transcendentals=0),
    )(scalars, *[piece for piece in coded for _ in range(kinds)], taps, decay, decay_block, coeff, skip)


def on_device(x_codes, w_codes, req_mult, req_shift, short_codes, residue_codes, rates, skip_gain):
    seq_devs = lax.axis_size("seq")
    tp_devs = lax.axis_size("tp")
    assert tp_devs == 4
    place = lax.axis_index("seq")
    layer = lax.axis_index("tp")
    outer = (layer == 0) | (layer == 3)
    rows_dev, features = x_codes.shape
    kinds, _, chan_seq = w_codes.shape
    states = rates.shape[0]
    half = chan_seq // 2
    width = math.gcd(half, 256)
    groups = half // width

    def swap(values, mask):
        return lax.ppermute(values, "seq", [(s, s ^ mask) for s in range(seq_devs)])

    own = x_codes.astype(jnp.bfloat16)
    far = {mask: swap(own, mask) for mask in range(2, seq_devs, 2)}
    blocks = {0: own, 1: swap(own, 1)}
    for mask in range(2, seq_devs, 2):
        blocks[mask] = swap(own, mask)
        blocks[mask + 1] = swap(blocks[mask], 1)

    requant = req_mult.astype(jnp.float32) * jnp.exp2(-req_shift.astype(jnp.float32))
    scale = (requant * WIRE_SCALE).reshape(kinds, 1, chan_seq)
    taps = short_codes.astype(jnp.float32) * (1.0 / 128.0)
    coeff = (
        residue_codes.astype(jnp.float32)
        * (1.0 / (127.0 * math.sqrt(states)))
        * jnp.sqrt(-jnp.expm1(-2.0 * rates))
    )
    decay = jnp.exp(-rates)
    decay_block = jnp.exp(-rates * rows_dev)
    skip = skip_gain.reshape(1, chan_seq)

    pairs = list(range(2, seq_devs // 2))
    pieces = [(g, q) for q in (0, 1) for g in range(groups)]
    pieces += [(g, q) for g in range(groups) for q in pairs]
    count = len(pieces)
    half_first = 1 - layer % 2
    half_second = layer % 2

    def partials(store, members, which, token):
        chosen, members = members
        taken = [blocks[2 * q + j] for q in members for j in range(2)]
        block = (which * groups + chosen[0]) // len(chosen)
        results = project(taken, w_codes, scale, block, len(chosen), width, token)
        store.update(zip([pieces.index((g, q)) for q in members for g in chosen], results))

    calls = {pieces.index((0, q)): (list(range(groups)), [q]) for q in (0, 1)}
    for g in range(groups):
        for i in range(0, len(pairs), 2):
            calls[pieces.index((g, pairs[i]))] = [g], pairs[i : i + 2]

    first, second = {}, {}
    got_outer, got_inner = {}, {}
    finals = {}
    token = jnp.zeros((8, LANES), jnp.float32)
    for g in range(groups):
        partials(first, ([g], [0]), half_first, token)
    gated = [None] * groups
    ready = [max(i for i, piece in enumerate(pieces) if piece[0] == g) + 3 for g in range(groups)]
    for t in range(count + 3):
        send_outer = send_inner = None
        if t < count + 2:
            if t < 2:
                send_outer = first[t]
            else:
                send_outer = first[t - 2] + got_inner[t - 1].astype(jnp.float32)
                if t < count:
                    send_outer = jnp.where(outer, first[t], send_outer)
            send_outer = send_outer.astype(WIRE)
        if t >= 1:
            if t < 3:
                mine = second[t - 1]
            elif t <= count:
                mine = jnp.where(outer, second[t - 3], second[t - 1])
            else:
                mine = second[t - 3]
            total = mine + got_outer[t - 1].astype(jnp.float32)
            if t <= count:
                send_inner = total.astype(WIRE)
            if t >= 3:
                finals[t - 3] = jnp.clip(total * (1.0 / WIRE_SCALE), -127.0, 127.0).astype(jnp.bfloat16)
        for g in range(groups):
            if t == ready[g] + 1 and send_outer is not None:
                send_outer, gated[g] = lax.optimization_barrier((send_outer, gated[g]))
        if send_inner is not None and send_outer is not None:
            send_outer, send_inner = lax.optimization_barrier((send_outer, send_inner))
        if send_outer is not None:
            got_outer[t] = lax.ppermute(send_outer, "tp", OUTER_PAIRS)
        if send_inner is not None:
            got_inner[t] = lax.ppermute(send_inner, "tp", INNER_PAIRS)
        if t in calls:
            partials(second, calls[t], half_second, blocks.get(6, token) if calls[t][1] == [1] else token)
        if t + 1 in calls:
            partials(first, calls[t + 1], half_first, blocks.get(4, token) if calls[t + 1][1] == [1] else token)
        for g in range(groups):
            members = [i for i, piece in enumerate(pieces) if piece[0] == g]
            if t == ready[g]:
                members = sorted(members, key=lambda i: pieces[i][1])
                coded = [finals[i] for i in members]
                column_start = (jnp.where(layer == 0, 0, groups) + g) * (width // LANES)
                gated[g] = hyena(coded, seq_devs, taps, decay, decay_block, coeff, skip, place, column_start)

    rows_out = rows_dev // tp_devs

    def spread(values):
        width = values.shape[2]
        parts = values.reshape(seq_devs, tp_devs, rows_out, width)
        step = jnp.where(layer < 2, 1, -1)

        def slice_for(distance):
            target = jnp.clip(layer + distance * step, 0, tp_devs - 1)
            return lax.dynamic_index_in_dim(parts, target, 1, keepdims=False)

        near = lax.ppermute(slice_for(1), "tp", OUTER_PAIRS)
        middle = lax.ppermute(slice_for(2), "tp", [(0, 2), (2, 0), (1, 3), (3, 1)])
        opposite = lax.ppermute(slice_for(3), "tp", [(0, 3), (3, 0)])
        kept = slice_for(0)
        low = jnp.where(layer == 0, kept, jnp.where(layer == 1, near, jnp.where(layer == 2, middle, opposite)))
        high = jnp.where(layer == 3, kept, jnp.where(layer == 2, near, jnp.where(layer == 1, middle, opposite)))
        return low, high

    halves = [spread(values) for values in gated]
    mine = jnp.concatenate([low for low, _ in halves] + [high for _, high in halves], axis=2)
    landed = lax.all_to_all(mine, "seq", split_axis=0, concat_axis=0, tiled=True)
    return jnp.transpose(landed, (1, 0, 2)).reshape(rows_out, seq_devs * chan_seq)


def solution(mesh):
    placed = (
        P("seq", "tp"),
        P(None, "tp", "seq"),
        P(None, "seq"),
        P(None, "seq"),
        P(None, None, "seq"),
        P(None, "seq"),
        P(None, "seq"),
        P("seq"),
    )
    return jax.shard_map(
        on_device, mesh=mesh, in_specs=placed, out_specs=P(("seq", "tp"), None), check_vma=False
    )
```
